512 devices in a mesh: row: 32 (over y, x), col: 16 (over z, core).
Axes of the slice: x: 4, y: 8, z: 8, core: 2. Of those that a mesh axis runs over, the one named last changes fastest.
Arguments:
- choi: float32 [4, 8192, 4096], P(None, 'row', 'col'), may hold values from -0.5 to 8, as said below
Outputs:
- factored: float32 [4, 8192, 4096], P(None, 'row', 'col')
The draws below stay inside these ranges and needn't reach their ends.
Inputs may be any that keep to these rules, and one draw needn't show every extreme that they name: `choi`: the leading 4096 x 4096 block of the matrix is symmetric with a positive diagonal, and its leading 2 * 256 square is positive definite.
All inputs are finite; a program needn't handle non-finite values.
Results may differ from the reference program's by a relative error of at most 0.0001.
Values sent between devices are 32-bit elements; how exact they have to be, the bound alone decides.
No kernel may reach another device: no remote copies, remote signals or barrier semaphores. Data moves between devices by JAX's collectives and lax.ppermute only.
A program may use at most 64 MiB of HBM per device.

```python
import math
import jax
import jax.numpy as jnp
from jax import lax

TILE = 256
RT_DEV = 4
PANELS = 2
ORDER = 32768
COLS = 4096
N_ROW = 32


off_spread = 0.04


def draw_choi(key, part):
    first = jax.random.fold_in(key, 11)
    second = jax.random.fold_in(key, 23)
    noise_draw = jax.random.normal(first, (ORDER, COLS), jnp.float32) * off_spread
    diag_draw = jax.random.uniform(second, (COLS,), jnp.float32, 4.5, 8.0)
    upper_part = noise_draw[:COLS]
    symmetric = (upper_part + upper_part.T) * math.sqrt(0.5)
    ident_mask = jnp.arange(COLS)[:, None] == jnp.arange(COLS)[None, :]
    symmetric = jnp.where(ident_mask, diag_draw[:, None], symmetric)
    whole_matrix = jnp.concatenate([symmetric, noise_draw[COLS:]], axis=0)
    return whole_matrix.reshape(RT_DEV, ORDER // RT_DEV, COLS)


def setup_inputs(seed: int = 0) -> dict:
    splits = jax.random.split(jax.random.key(seed), 2)
    return {
        "choi": draw_choi(jax.random.fold_in(splits[1], 71), 0),
    }


def reference(choi):
    matrix = choi.reshape(RT_DEV * N_ROW * TILE, COLS)
    identity = jnp.eye(TILE, dtype=matrix.dtype)
    for step in range(PANELS):
        start = step * TILE
        finish = start + TILE
        factor = jnp.linalg.cholesky(matrix[start:finish, start:finish])
        inverse = jax.scipy.linalg.solve_triangular(factor, identity, lower=True)
        beneath = jnp.dot(matrix[finish:, start:finish], inverse.T, precision=lax.Precision.HIGHEST)
        column = jnp.concatenate([jnp.zeros((start, TILE), matrix.dtype), factor, beneath], axis=0)
        matrix = matrix.at[:, start:finish].set(column)
        change = jnp.dot(beneath, beneath[:COLS - finish].T, precision=lax.Precision.HIGHEST)
        matrix = matrix.at[finish:, finish:].add(-change)
    matrix = matrix.at[:PANELS * TILE, PANELS * TILE:].set(0.0)
    return matrix.reshape(RT_DEV, N_ROW * TILE, COLS)
```

```python
import jax
import jax.numpy as jnp
from jax import lax
from jax.sharding import Mesh
from jax.sharding import PartitionSpec as P

PANELS = 2
HIGHEST = lax.Precision.HIGHEST
ROW = ("y", "x")
COL = ("z", "core")


def doubling(block, axis, size):
    place = lax.axis_index(axis)
    step = size // 2
    while step:
        pairs = [(i, i + step) for i in range(0, size, 2 * step)]
        sent = lax.ppermute(block, axis, pairs)
        block = jnp.where(place % (2 * step) == step, sent, block)
        step //= 2
    return block


def panels_of(choi):
    slots, tile, _ = choi.shape
    deep = lax.axis_size("z")
    flat = choi.reshape(deep, slots * tile // deep, tile)
    piece = jnp.where(lax.axis_index("z") == 0, flat[0], 0.0)
    for z in range(1, deep):
        piece = piece + lax.ppermute(flat[z], "z", [(0, z)])
    whole = lax.all_gather(piece, COL)
    whole = whole.reshape(deep, 2, *piece.shape)
    return jnp.concatenate(
        [whole[:, k].reshape(slots * tile, tile) for k in range(PANELS)], axis=1
    )


def top_rows(choi):
    tile = choi.shape[1]
    high = lax.axis_size("y")
    x = lax.axis_index("x")
    core = lax.axis_index("core")
    part = tile // high
    mine = lax.all_to_all(choi[0].reshape(high, part, tile), "y", 0, 0)[0]
    other = lax.ppermute(mine, "x", [(0, 1), (1, 0)])
    both = jnp.where(x == 0, jnp.concatenate([mine, other]), jnp.concatenate([other, mine]))
    both = jnp.where(x < 2, both, lax.ppermute(both, "x", [(0, 3), (1, 2)]))
    lead = doubling(both, "z", lax.axis_size("z"))
    sent = jnp.concatenate([both, lead])
    got = lax.all_to_all(jnp.broadcast_to(sent, (high, *sent.shape)), "y", 0, 0)
    got = got.reshape(high, 4, part, tile).transpose(1, 0, 2, 3).reshape(2, 2 * tile, tile)
    column, half = got[0], got[1]
    pair = lax.ppermute(half, "core", [(0, 1), (1, 0)])
    lead = jnp.where(
        core == 0,
        jnp.concatenate([half, pair], axis=1),
        jnp.concatenate([pair, half], axis=1),
    )
    return column, lead


def factor_of(lead):
    factor = jnp.linalg.cholesky(lead)
    identity = jnp.eye(lead.shape[0], dtype=jnp.float32)
    inverse = jax.scipy.linalg.solve_triangular(factor, identity, lower=True)
    return factor, inverse


def body(choi):
    slots, tile, _ = choi.shape
    row = lax.axis_index(ROW)
    col = lax.axis_index(COL)
    panels = panels_of(choi)
    column, lead = top_rows(choi)
    factor, inverse = factor_of(lead)
    in_panel = col < PANELS
    half = jnp.dot(inverse, column, precision=HIGHEST)
    identity = jnp.eye(2 * tile, dtype=jnp.float32)
    place = jnp.minimum(col, PANELS - 1) * tile
    chosen = lax.dynamic_slice(identity, (0, place), (2 * tile, tile))
    half = jnp.where(in_panel, -chosen, half)
    weight = lax.dot_general(
        inverse, half, (((0,), (0,)), ((), ())), precision=HIGHEST
    )
    base = jnp.where(in_panel, 0.0, choi)
    change = jnp.dot(panels, weight, precision=HIGHEST).reshape(choi.shape)
    result = base - change
    corner = lax.dynamic_slice(
        factor, (jnp.minimum(row, PANELS - 1) * tile, place), (tile, tile)
    )
    corner = jnp.where(in_panel, corner, 0.0)
    slot = jnp.arange(slots)[:, None, None]
    return jnp.where((slot == 0) & (row < PANELS), corner[None], result)


def solution(mesh):
    finer = Mesh(mesh.devices.reshape(8, 4, 8, 2), ("y", "x", "z", "core"))
    spec = P(None, ROW, COL)
    return jax.shard_map(
        body, mesh=finer, in_specs=(spec,), out_specs=spec, check_vma=False
    )
```

```python
import jax
import jax.numpy as jnp
from jax import lax
from jax.experimental import pallas as pl
from jax.experimental.pallas import tpu as pltpu
from jax.sharding import Mesh
from jax.sharding import PartitionSpec as P

PANELS = 2
HIGHEST = lax.Precision.HIGHEST
STEPS = 40
LAST = 5e-4
ROW = ("y", "x")
COL = ("z", "core")


def doubling(block, axis, size):
    place = lax.axis_index(axis)
    step = size // 2
    while step:
        pairs = [(i, i + step) for i in range(0, size, 2 * step)]
        sent = lax.ppermute(block, axis, pairs)
        block = jnp.where(place % (2 * step) == step, sent, block)
        step //= 2
    return block


def panels_of(choi):
    slots, tile, _ = choi.shape
    deep = lax.axis_size("z")
    flat = choi.reshape(deep, slots * tile // deep, tile)
    piece = jnp.where(lax.axis_index("z") == 0, flat[0], 0.0)
    for z in range(1, deep):
        piece = piece + lax.ppermute(flat[z], "z", [(0, z)])
    whole = lax.all_gather(piece, COL)
    whole = whole.reshape(deep, 2, *piece.shape)
    return jnp.concatenate(
        [whole[:, k].reshape(slots * tile, tile) for k in range(PANELS)], axis=1
    )


def top_rows(choi):
    tile = choi.shape[1]
    high = lax.axis_size("y")
    x = lax.axis_index("x")
    core = lax.axis_index("core")
    part = tile // high
    mine = lax.all_to_all(choi[0].reshape(high, part, tile), "y", 0, 0)[0]
    other = lax.ppermute(mine, "x", [(0, 1), (1, 0)])
    both = jnp.where(x == 0, jnp.concatenate([mine, other]), jnp.concatenate([other, mine]))
    both = jnp.where(x < 2, both, lax.ppermute(both, "x", [(0, 3), (1, 2)]))
    lead = doubling(both, "z", lax.axis_size("z"))
    sent = jnp.concatenate([both, lead])
    got = lax.all_to_all(jnp.broadcast_to(sent, (high, *sent.shape)), "y", 0, 0)
    got = got.reshape(high, 4, part, tile).transpose(1, 0, 2, 3).reshape(2, 2 * tile, tile)
    column, half = got[0], got[1]
    pair = lax.ppermute(half, "core", [(0, 1), (1, 0)])
    lead = jnp.where(
        core == 0,
        jnp.concatenate([half, pair], axis=1),
        jnp.concatenate([pair, half], axis=1),
    )
    return column, lead


def product(left, right, contract=((1,), (0,)), precision=HIGHEST):
    return lax.dot_general(
        left, right, (contract, ((), ())), precision=precision,
        preferred_element_type=jnp.float32,
    )


def square(block):
    return jnp.sum(block * block)


def eliminate(lead_ref, inverse_ref, work_ref):
    order = lead_ref.shape[0]
    rows = lax.broadcasted_iota(jnp.int32, (order, order), 0)
    cols = lax.broadcasted_iota(jnp.int32, (order, order), 1)
    work_ref[...] = lead_ref[...]
    inverse_ref[...] = (rows == cols).astype(jnp.float32)

    def pivot(k, carry):
        work = work_ref[...]
        column = jnp.sum(jnp.where(cols == k, work, 0.0), axis=1, keepdims=True)
        place = lax.broadcasted_iota(jnp.int32, (order, 1), 0)
        corner = jnp.sum(jnp.where(place == k, column, 0.0))
        scale = jnp.full((order, 1), corner)
        ratio = jnp.where(place > k, column / scale, 0.0)
        work_ref[...] = work - ratio * work_ref[pl.ds(k, 1), :]
        inverse = inverse_ref[...] - ratio * inverse_ref[pl.ds(k, 1), :]
        inverse_ref[...] = jnp.where(place == k, inverse / jnp.sqrt(scale), inverse)
        return carry

    lax.fori_loop(0, order, pivot, 0)


def factor_kernel(lead_ref, inverse_ref, factor_ref, work_ref):
    order = lead_ref.shape[0]
    half = order // 2
    rows = lax.broadcasted_iota(jnp.int32, (order, order), 0)
    cols = lax.broadcasted_iota(jnp.int32, (order, order), 1)
    same = rows == cols
    lead = lead_ref[...]
    down = lax.rsqrt(jnp.sum(jnp.where(same, lead, 0.0), axis=1, keepdims=True))
    along = lax.rsqrt(jnp.sum(jnp.where(same, lead, 0.0), axis=0, keepdims=True))
    scaled = lead * down * along
    off = jnp.where(same, 0.0, scaled).astype(jnp.bfloat16)
    twice = product(off, off, precision=None)
    bound = jnp.sqrt(jnp.sqrt(jnp.full((1, 1), square(twice))))
    shrink = jnp.where(bound < 1.0, jnp.ones_like(bound), 1.0 / (1.0 + bound))
    first = jnp.where(rows > cols, -scaled * shrink, jnp.where(same, 1.5 - 0.5 * shrink, 0.0))
    inverse_ref[...] = first * along * jnp.sqrt(shrink)

    top, low = pl.ds(0, half), pl.ds(half, half)
    small_rows = rows[:half, :half]
    small_cols = cols[:half, :half]
    unit = (small_rows == small_cols).astype(jnp.float32)
    across = ((1,), (1,))

    def lower(block):
        return jnp.where(small_rows > small_cols, block, 0.5 * unit * block)

    def unfinished(carry):
        count, residual = carry
        return (count < STEPS) & (residual > LAST)

    def newton(carry):
        count, _ = carry
        x00, x10, x11 = inverse_ref[top, top], inverse_ref[low, top], inverse_ref[low, low]
        s00, s10 = lead_ref[top, top], lead_ref[low, top]
        s01, s11 = lead_ref[top, low], lead_ref[low, low]
        y00 = product(x00, s00)
        y10 = product(x10, s00) + product(x11, s10)
        y11 = product(x10, s01) + product(x11, s11)
        e00 = product(y00, x00, across) - unit
        e10 = product(y10, x00, across)
        e11 = product(y10, x10, across) + product(y11, x11, across) - unit
        residual = jnp.sqrt(square(e00) + 2.0 * square(e10) + square(e11))
        f00, f11 = lower(e00), lower(e11)
        inverse_ref[top, top] = x00 - product(f00, x00)
        inverse_ref[low, top] = x10 - product(e10, x00) - product(f11, x10)
        inverse_ref[low, low] = x11 - product(f11, x11)
        return count + 1, residual

    _, residual = lax.while_loop(unfinished, newton, (jnp.int32(0), jnp.float32(1.0)))

    @pl.when(jnp.logical_not(residual <= LAST))
    def _():
        eliminate(lead_ref, inverse_ref, work_ref)

    factor = product(lead_ref[...], inverse_ref[...], across)
    factor_ref[...] = jnp.where(rows >= cols, factor, 0.0)


def factor_of(lead):
    shape = jax.ShapeDtypeStruct(lead.shape, jnp.float32)
    inverse, factor = pl.pallas_call(
        factor_kernel,
        out_shape=(shape, shape),
        scratch_shapes=[pltpu.VMEM(lead.shape, jnp.float32)],
        compiler_params=pltpu.CompilerParams(vmem_limit_bytes=40 * 2**20),
        cost_estimate=pl.CostEstimate(
            flops=20 * lead.shape[0] ** 3, bytes_accessed=12 * lead.size, transcendentals=0
        ),
    )(lead)
    return factor, inverse


def body(choi):
    slots, tile, _ = choi.shape
    row = lax.axis_index(ROW)
    col = lax.axis_index(COL)
    panels = panels_of(choi)
    column, lead = top_rows(choi)
    factor, inverse = factor_of(lead)
    in_panel = col < PANELS
    half = jnp.dot(inverse, column, precision=HIGHEST)
    identity = jnp.eye(2 * tile, dtype=jnp.float32)
    place = jnp.minimum(col, PANELS - 1) * tile
    chosen = lax.dynamic_slice(identity, (0, place), (2 * tile, tile))
    half = jnp.where(in_panel, -chosen, half)
    weight = lax.dot_general(
        inverse, half, (((0,), (0,)), ((), ())), precision=HIGHEST
    )
    base = jnp.where(in_panel, 0.0, choi)
    change = jnp.dot(panels, weight, precision=HIGHEST).reshape(choi.shape)
    result = base - change
    corner = lax.dynamic_slice(
        factor, (jnp.minimum(row, PANELS - 1) * tile, place), (tile, tile)
    )
    corner = jnp.where(in_panel, corner, 0.0)
    slot = jnp.arange(slots)[:, None, None]
    return jnp.where((slot == 0) & (row < PANELS), corner[None], result)


def solution(mesh):
    finer = Mesh(mesh.devices.reshape(8, 4, 8, 2), ("y", "x", "z", "core"))
    spec = P(None, ROW, COL)
    return jax.shard_map(
        body, mesh=finer, in_specs=(spec,), out_specs=spec, check_vma=False
    )
```

```python
import jax
import jax.numpy as jnp
from jax import lax
from jax.experimental import pallas as pl
from jax.experimental.pallas import tpu as pltpu
from jax.sharding import Mesh
from jax.sharding import PartitionSpec as P

PANELS = 2
HIGHEST = lax.Precision.HIGHEST
STEPS = 40
FAR_STEPS = 6
NEAR = 0.1
LAST = 5e-4
ROW = ("y", "x")
COL = ("z", "core")


together = lax.optimization_barrier


def doubled(block, axis, step):
    size = lax.axis_size(axis)
    pairs = [(i, i + step) for i in range(0, size, 2 * step)]
    sent = lax.ppermute(block, axis, pairs)
    return jnp.where(lax.axis_index(axis) % (2 * step) == step, sent, block)


def scattered(block, axis):
    size = lax.axis_size(axis)
    parts = jnp.split(block, size)
    mine = jnp.where(lax.axis_index(axis) == 0, parts[0], 0.0)
    for i in range(1, size):
        mine = mine + lax.ppermute(parts[i], axis, [(0, i)])
    return mine


def gathered(block, axis):
    copies = jnp.broadcast_to(block, (lax.axis_size(axis), *block.shape))
    return lax.all_to_all(copies, axis, 0, 0)


def from_two(mine):
    x = lax.axis_index("x")
    near = lax.ppermute(mine, "x", [(0, 1), (1, 0)])
    even = lax.ppermute(mine, "x", [(0, 2), (1, 3)])
    odd = lax.ppermute(mine, "x", [(0, 3), (1, 2)])
    first = jnp.where(x == 0, mine, jnp.where(x == 1, near, jnp.where(x == 2, even, odd)))
    second = jnp.where(x == 1, mine, jnp.where(x == 0, near, jnp.where(x == 3, even, odd)))
    return jnp.concatenate([first, second])


def spread(choi):
    slots, tile, _ = choi.shape
    high = lax.axis_size("y")
    core = lax.axis_index("core")
    top = lax.all_to_all(choi[0].reshape(high, tile // high, tile), "y", 0, 0)[0]
    panel = scattered(choi.reshape(slots * tile, tile), "z")
    top = from_two(top)
    panel, top = together((panel, top))
    panels = lax.all_gather(panel, COL)
    lead = doubled(doubled(doubled(top, "z", 4), "z", 2), "z", 1)
    parts = gathered(jnp.concatenate([top, lead]), "y")
    parts = parts.reshape(high, 2 * PANELS, tile // high, tile).transpose(1, 0, 2, 3)
    column, half = parts.reshape(2, PANELS * tile, tile)
    pair = lax.ppermute(half, "core", [(0, 1), (1, 0)])
    left, right = jnp.where(core == 0, half, pair), jnp.where(core == 0, pair, half)
    lead = jnp.concatenate([left, right], axis=1)
    return column, lead, panels


def product(left, right, contract=((1,), (0,)), precision=HIGHEST):
    return lax.dot_general(
        left, right, (contract, ((), ())), precision=precision,
        preferred_element_type=jnp.float32,
    )


def rough(left, right, contract=((1,), (0,))):
    low = jnp.bfloat16
    left_high, right_high = left.astype(low), right.astype(low)
    left_rest = (left - left_high.astype(jnp.float32)).astype(low)
    right_rest = (right - right_high.astype(jnp.float32)).astype(low)
    small = product(left_high, right_rest, contract, None)
    small = small + product(left_rest, right_high, contract, None)
    return small + product(left_high, right_high, contract, None)


def square(block):
    return jnp.sum(block * block)


def eliminate(lead_ref, inverse_ref, work_ref):
    order = lead_ref.shape[0]
    rows = lax.broadcasted_iota(jnp.int32, (order, order), 0)
    cols = lax.broadcasted_iota(jnp.int32, (order, order), 1)
    work_ref[...] = lead_ref[...]
    inverse_ref[...] = (rows == cols).astype(jnp.float32)

    def pivot(k, carry):
        work = work_ref[...]
        column = jnp.sum(jnp.where(cols == k, work, 0.0), axis=1, keepdims=True)
        place = lax.broadcasted_iota(jnp.int32, (order, 1), 0)
        corner = jnp.sum(jnp.where(place == k, column, 0.0))
        scale = jnp.full((order, 1), corner)
        ratio = jnp.where(place > k, column / scale, 0.0)
        work_ref[...] = work - ratio * work_ref[pl.ds(k, 1), :]
        inverse = inverse_ref[...] - ratio * inverse_ref[pl.ds(k, 1), :]
        inverse_ref[...] = jnp.where(place == k, inverse / jnp.sqrt(scale), inverse)
        return carry

    lax.fori_loop(0, order, pivot, 0)


def weight_kernel(place_ref, lead_ref, column_ref, weight_ref, corner_ref, inverse_ref, work_ref):
    order = lead_ref.shape[0]
    half = order // 2
    rows = lax.broadcasted_iota(jnp.int32, (order, order), 0)
    cols = lax.broadcasted_iota(jnp.int32, (order, order), 1)
    same = rows == cols
    lead = lead_ref[...]
    down = lax.rsqrt(jnp.sum(jnp.where(same, lead, 0.0), axis=1, keepdims=True))
    along = lax.rsqrt(jnp.sum(jnp.where(same, lead, 0.0), axis=0, keepdims=True))
    scaled = lead * down * along
    off = jnp.where(same, 0.0, scaled).astype(jnp.bfloat16)
    twice = product(off, off, precision=None)
    bound = jnp.sqrt(jnp.sqrt(jnp.full((1, 1), square(twice))))
    shrink = jnp.where(bound < 1.0, jnp.ones_like(bound), 1.0 / (1.0 + bound))
    first = jnp.where(rows > cols, -scaled * shrink, jnp.where(same, 1.5 - 0.5 * shrink, 0.0))
    inverse_ref[...] = first * along * jnp.sqrt(shrink)

    top, low = pl.ds(0, half), pl.ds(half, half)
    small_rows = rows[:half, :half]
    small_cols = cols[:half, :half]
    unit = (small_rows == small_cols).astype(jnp.float32)
    across = ((1,), (1,))

    def lower(block):
        return jnp.where(small_rows > small_cols, block, 0.5 * unit * block)

    def step(multiply):
        x00, x10, x11 = inverse_ref[top, top], inverse_ref[low, top], inverse_ref[low, low]
        s00, s10 = lead_ref[top, top], lead_ref[low, top]
        s01, s11 = lead_ref[top, low], lead_ref[low, low]
        y00 = multiply(x00, s00)
        y10 = multiply(x10, s00) + multiply(x11, s10)
        y11 = multiply(x10, s01) + multiply(x11, s11)
        e00 = multiply(y00, x00, across) - unit
        e10 = multiply(y10, x00, across)
        e11 = multiply(y10, x10, across) + multiply(y11, x11, across) - unit
        residual = jnp.sqrt(square(e00) + 2.0 * square(e10) + square(e11))
        f00, f11 = lower(e00), lower(e11)
        inverse_ref[top, top] = x00 - multiply(f00, x00)
        inverse_ref[low, top] = x10 - multiply(e10, x00) - multiply(f11, x10)
        inverse_ref[low, low] = x11 - multiply(f11, x11)
        return residual

    def far(carry):
        count, residual = carry
        return (count < FAR_STEPS) & (residual > NEAR)

    def unfinished(carry):
        count, residual = carry
        return (count < STEPS) & (residual > LAST)

    start = (jnp.int32(0), jnp.float32(1.0))
    count, _ = lax.while_loop(far, lambda carry: (carry[0] + 1, step(rough)), start)
    start = (count, jnp.float32(1.0))
    _, residual = lax.while_loop(
        unfinished, lambda carry: (carry[0] + 1, step(product)), start
    )

    @pl.when(jnp.logical_not(residual <= LAST))
    def _():
        eliminate(lead_ref, inverse_ref, work_ref)

    x00, x10, x11 = inverse_ref[top, top], inverse_ref[low, top], inverse_ref[low, low]
    row, col = place_ref[0], place_ref[1]
    down = ((0,), (0,))

    @pl.when(col >= PANELS)
    def _():
        r0, r1 = column_ref[top, :], column_ref[low, :]
        h0 = product(x00, r0)
        h1 = product(x10, r0) + product(x11, r1)
        weight_ref[top, :] = product(x00, h0, down) + product(x10, h1, down)
        weight_ref[low, :] = product(x11, h1, down)
        corner_ref[...] = jnp.zeros((half, half), jnp.float32)

    @pl.when(col == 0)
    def _():
        weight_ref[top, :] = -x00.T
        weight_ref[low, :] = jnp.zeros((half, half), jnp.float32)
        corner = product(lead_ref[pl.ds(pl.multiple_of(jnp.minimum(row, 1) * half, half), half), top], x00, across)
        corner_ref[...] = jnp.where((row > 0) | (small_rows >= small_cols), corner, 0.0)

    @pl.when(col == 1)
    def _():
        weight_ref[top, :] = -x10.T
        weight_ref[low, :] = -x11.T
        corner = product(lead_ref[low, top], x10, across) + product(lead_ref[low, low], x11, across)
        corner_ref[...] = jnp.where((row > 0) & (small_rows >= small_cols), corner, 0.0)


def update_kernel(place_ref, panels_ref, weight_ref, corner_ref, choi_ref, out_ref):
    tile = out_ref.shape[1]
    row, col = place_ref[0], place_ref[1]
    top = (pl.program_id(0) == 0) & (row < PANELS)

    @pl.when(top)
    def _():
        out_ref[0] = corner_ref[...]

    @pl.when(jnp.logical_not(top))
    def _():
        base = jnp.where(col < PANELS, 0.0, choi_ref[0])
        for k in range(PANELS):
            panel = panels_ref[:, k].reshape(tile, tile)
            base = base - product(panel, weight_ref[pl.ds(k * tile, tile), :])
        out_ref[0] = base


def body(choi):
    slots, tile, _ = choi.shape
    order = PANELS * tile
    place = jnp.stack([lax.axis_index(ROW), lax.axis_index(COL)]).astype(jnp.int32)
    column, lead, panels = spread(choi)
    scalars = pl.BlockSpec(memory_space=pltpu.SMEM)
    vector = pl.BlockSpec(memory_space=pltpu.VMEM)
    weight, corner = pl.pallas_call(
        weight_kernel,
        in_specs=[scalars, vector, vector],
        out_shape=(
            jax.ShapeDtypeStruct((order, tile), jnp.float32),
            jax.ShapeDtypeStruct((tile, tile), jnp.float32),
        ),
        scratch_shapes=[pltpu.VMEM((order, order), jnp.float32)] * 2,
        compiler_params=pltpu.CompilerParams(vmem_limit_bytes=24 * 2**20),
        cost_estimate=pl.CostEstimate(
            flops=20 * order**3, bytes_accessed=12 * order * order, transcendentals=0
        ),
    )(place, lead, column)
    deep = panels.shape[0] // PANELS
    panels = panels.reshape(deep, PANELS, *panels.shape[1:])
    part = (deep // slots, *panels.shape[1:])
    one = pl.BlockSpec((1, tile, tile), lambda s: (s, 0, 0))
    return pl.pallas_call(
        update_kernel,
        grid=(slots,),
        in_specs=[
            scalars,
            pl.BlockSpec(part, lambda s: (s, 0, 0, 0)),
            pl.BlockSpec((order, tile), lambda s: (0, 0)),
            pl.BlockSpec((tile, tile), lambda s: (0, 0)),
            one,
        ],
        out_specs=one,
        out_shape=jax.ShapeDtypeStruct(choi.shape, jnp.float32),
        compiler_params=pltpu.CompilerParams(vmem_limit_bytes=16 * 2**20),
    )(place, panels, weight, corner, choi)


def solution(mesh):
    finer = Mesh(mesh.devices.reshape(8, 4, 8, 2), ("y", "x", "z", "core"))
    spec = P(None, ROW, COL)
    return jax.shard_map(
        body, mesh=finer, in_specs=(spec,), out_specs=spec, check_vma=False
    )
```

```python
import jax
import jax.numpy as jnp
from jax import lax
from jax.experimental import pallas as pl
from jax.experimental.pallas import tpu as pltpu
from jax.sharding import Mesh
from jax.sharding import PartitionSpec as P

PANELS = 2
HIGHEST = lax.Precision.HIGHEST
STEPS = 40
FAR_STEPS = 6
NEAR = 0.1
LAST = 5e-4
ROW = ("y", "x")
COL = ("z", "core")


together = lax.optimization_barrier


def doubled(block, axis, step):
    size = lax.axis_size(axis)
    pairs = [(i, i + step) for i in range(0, size, 2 * step)]
    sent = lax.ppermute(block, axis, pairs)
    return jnp.where(lax.axis_index(axis) % (2 * step) == step, sent, block)


def scattered(block, axis):
    size = lax.axis_size(axis)
    parts = jnp.split(block, size // 2)
    mine = jnp.where(lax.axis_index(axis) == 0, parts[0], 0.0)
    for i in range(1, size // 2):
        mine = mine + lax.ppermute(parts[i], axis, [(0, 2 * i)])
    return mine


def halved(block, axis):
    size = lax.axis_size(axis)
    keep, give = jnp.split(block, 2)
    sent = lax.ppermute(give, axis, [(i, i + 1) for i in range(0, size, 2)])
    return jnp.where(lax.axis_index(axis) % 2 == 1, sent, keep)


def gathered(block, axis):
    copies = jnp.broadcast_to(block, (lax.axis_size(axis), *block.shape))
    return lax.all_to_all(copies, axis, 0, 0)


def from_two(mine):
    x = lax.axis_index("x")
    near = lax.ppermute(mine, "x", [(0, 1), (1, 0)])
    even = lax.ppermute(mine, "x", [(0, 2), (1, 3)])
    odd = lax.ppermute(mine, "x", [(0, 3), (1, 2)])
    first = jnp.where(x == 0, mine, jnp.where(x == 1, near, jnp.where(x == 2, even, odd)))
    second = jnp.where(x == 1, mine, jnp.where(x == 0, near, jnp.where(x == 3, even, odd)))
    return jnp.concatenate([first, second])


def stacked(parts, tile):
    high, double, width = parts.shape
    parts = parts.reshape(high, 2, double // 2, width).transpose(1, 0, 2, 3)
    return parts.reshape(2 * tile, width)


def spread(choi):
    slots, tile, _ = choi.shape
    high = lax.axis_size("y")
    core = lax.axis_index("core")
    top = lax.all_to_all(choi[0].reshape(high, tile // high, tile), "y", 0, 0)[0]
    panel = scattered(choi.reshape(slots * tile, tile), "z")
    top = from_two(top)
    panel, top = together((panel, top))
    panel = halved(panel, "z")
    lead = doubled(top, "z", 4)
    panel, lead = together((panel, lead))
    panels = lax.all_gather(panel, COL)
    column = gathered(top, "y")
    lead = doubled(doubled(lead, "z", 2), "z", 1)
    lead, column = together((lead, column))
    lead = gathered(lead, "y")
    column, half = stacked(column, tile), stacked(lead, tile)
    pair = lax.ppermute(half, "core", [(0, 1), (1, 0)])
    left, right = jnp.where(core == 0, half, pair), jnp.where(core == 0, pair, half)
    lead = jnp.concatenate([left, right], axis=1)
    return column, lead, panels


def product(left, right, contract=((1,), (0,)), precision=HIGHEST):
    return lax.dot_general(
        left, right, (contract, ((), ())), precision=precision,
        preferred_element_type=jnp.float32,
    )


def coarse(left, right, contract=((1,), (0,))):
    return product(left.astype(jnp.bfloat16), right.astype(jnp.bfloat16), contract, None)


def rough(left, right, contract=((1,), (0,))):
    low = jnp.bfloat16
    left_high, right_high = left.astype(low), right.astype(low)
    left_rest = (left - left_high.astype(jnp.float32)).astype(low)
    right_rest = (right - right_high.astype(jnp.float32)).astype(low)
    small = product(left_high, right_rest, contract, None)
    small = small + product(left_rest, right_high, contract, None)
    return small + product(left_high, right_high, contract, None)


def square(block):
    return jnp.sum(block * block)


def eliminate(lead_ref, inverse_ref, work_ref):
    order = lead_ref.shape[0]
    rows = lax.broadcasted_iota(jnp.int32, (order, order), 0)
    cols = lax.broadcasted_iota(jnp.int32, (order, order), 1)
    work_ref[...] = lead_ref[...]
    inverse_ref[...] = (rows == cols).astype(jnp.float32)

    def pivot(k, carry):
        work = work_ref[...]
        column = jnp.sum(jnp.where(cols == k, work, 0.0), axis=1, keepdims=True)
        place = lax.broadcasted_iota(jnp.int32, (order, 1), 0)
        corner = jnp.sum(jnp.where(place == k, column, 0.0))
        scale = jnp.full((order, 1), corner)
        ratio = jnp.where(place > k, column / scale, 0.0)
        work_ref[...] = work - ratio * work_ref[pl.ds(k, 1), :]
        inverse = inverse_ref[...] - ratio * inverse_ref[pl.ds(k, 1), :]
        inverse_ref[...] = jnp.where(place == k, inverse / jnp.sqrt(scale), inverse)
        return carry

    lax.fori_loop(0, order, pivot, 0)


def update_kernel(
    place_ref, lead_ref, column_ref, panels_ref, choi_ref, out_ref, inverse_ref, work_ref, weight_ref, corner_ref
):
    order = lead_ref.shape[0]
    half = order // 2
    rows = lax.broadcasted_iota(jnp.int32, (order, order), 0)
    cols = lax.broadcasted_iota(jnp.int32, (order, order), 1)
    same = rows == cols
    lead = lead_ref[...]
    down = lax.rsqrt(jnp.sum(jnp.where(same, lead, 0.0), axis=1, keepdims=True))
    along = lax.rsqrt(jnp.sum(jnp.where(same, lead, 0.0), axis=0, keepdims=True))
    scaled = lead * down * along
    off = jnp.where(same, 0.0, scaled).astype(jnp.bfloat16)
    twice = product(off, off, precision=None)
    bound = jnp.sqrt(jnp.sqrt(jnp.full((1, 1), square(twice))))
    shrink = jnp.where(bound < 1.0, jnp.ones_like(bound), 1.0 / (1.0 + bound))
    first = jnp.where(rows > cols, -scaled * shrink, jnp.where(same, 1.5 - 0.5 * shrink, 0.0))
    inverse_ref[...] = first * along * jnp.sqrt(shrink)

    top, low = pl.ds(0, half), pl.ds(half, half)
    small_rows = rows[:half, :half]
    small_cols = cols[:half, :half]
    unit = (small_rows == small_cols).astype(jnp.float32)
    across = ((1,), (1,))

    def lower(block):
        return jnp.where(small_rows > small_cols, block, 0.5 * unit * block)

    def step(multiply):
        x00, x10, x11 = inverse_ref[top, top], inverse_ref[low, top], inverse_ref[low, low]
        s00, s10 = lead_ref[top, top], lead_ref[low, top]
        s01, s11 = lead_ref[top, low], lead_ref[low, low]
        y00 = multiply(x00, s00)
        y10 = multiply(x10, s00) + multiply(x11, s10)
        y11 = multiply(x10, s01) + multiply(x11, s11)
        e00 = multiply(y00, x00, across) - unit
        e10 = multiply(y10, x00, across)
        e11 = multiply(y10, x10, across) + multiply(y11, x11, across) - unit
        residual = jnp.sqrt(square(e00) + 2.0 * square(e10) + square(e11))
        f00, f11 = lower(e00), lower(e11)
        inverse_ref[top, top] = x00 - multiply(f00, x00)
        inverse_ref[low, top] = x10 - multiply(e10, x00) - multiply(f11, x10)
        inverse_ref[low, low] = x11 - multiply(f11, x11)
        return residual

    def far(carry):
        count, residual = carry
        return (count < FAR_STEPS) & (residual > NEAR)

    def unfinished(carry):
        count, residual = carry
        return (count < STEPS) & (residual > LAST)

    start = (jnp.int32(1), step(coarse))
    count, _ = lax.while_loop(far, lambda carry: (carry[0] + 1, step(rough)), start)
    start = (count, jnp.float32(1.0))
    _, residual = lax.while_loop(
        unfinished, lambda carry: (carry[0] + 1, step(product)), start
    )

    @pl.when(jnp.logical_not(residual <= LAST))
    def _():
        eliminate(lead_ref, inverse_ref, work_ref)

    x00, x10, x11 = inverse_ref[top, top], inverse_ref[low, top], inverse_ref[low, low]
    row, col = place_ref[0], place_ref[1]
    down = ((0,), (0,))

    @pl.when(col >= PANELS)
    def _():
        r0, r1 = column_ref[top, :], column_ref[low, :]
        h0 = product(x00, r0)
        h1 = product(x10, r0) + product(x11, r1)
        weight_ref[top, :] = product(x00, h0, down) + product(x10, h1, down)
        weight_ref[low, :] = product(x11, h1, down)
        corner_ref[...] = jnp.zeros((half, half), jnp.float32)

    @pl.when(col == 0)
    def _():
        weight_ref[top, :] = -x00.T
        weight_ref[low, :] = jnp.zeros((half, half), jnp.float32)
        corner = product(lead_ref[pl.ds(pl.multiple_of(jnp.minimum(row, 1) * half, half), half), top], x00, across)
        corner_ref[...] = jnp.where((row > 0) | (small_rows >= small_cols), corner, 0.0)

    @pl.when(col == 1)
    def _():
        weight_ref[top, :] = -x10.T
        weight_ref[low, :] = -x11.T
        corner = product(lead_ref[low, top], x10, across) + product(lead_ref[low, low], x11, across)
        corner_ref[...] = jnp.where((row > 0) & (small_rows >= small_cols), corner, 0.0)

    for slot in range(choi_ref.shape[0]):
        base = jnp.where(col < PANELS, 0.0, choi_ref[slot])
        for k in range(PANELS):
            panel = panels_ref[slot, :, k].reshape(half, half)
            base = base - product(panel, weight_ref[pl.ds(k * half, half), :])
        out_ref[slot] = base

    @pl.when(row < PANELS)
    def _():
        out_ref[0] = corner_ref[...]


def body(choi):
    slots, tile, _ = choi.shape
    order = PANELS * tile
    place = jnp.stack([lax.axis_index(ROW), lax.axis_index(COL)]).astype(jnp.int32)
    column, lead, panels = spread(choi)
    deep = panels.shape[0] // PANELS
    panels = panels.reshape(slots, deep // slots, PANELS, *panels.shape[1:])
    vector = pl.BlockSpec(memory_space=pltpu.VMEM)
    return pl.pallas_call(
        update_kernel,
        in_specs=[pl.BlockSpec(memory_space=pltpu.SMEM)] + [vector] * 4,
        out_specs=vector,
        out_shape=jax.ShapeDtypeStruct(choi.shape, jnp.float32),
        scratch_shapes=[
            pltpu.VMEM((order, order), jnp.float32),
            pltpu.VMEM((order, order), jnp.float32),
            pltpu.VMEM((order, tile), jnp.float32),
            pltpu.VMEM((tile, tile), jnp.float32),
        ],
        compiler_params=pltpu.CompilerParams(vmem_limit_bytes=32 * 2**20),
    )(place, lead, column, panels, choi)


def solution(mesh):
    finer = Mesh(mesh.devices.reshape(8, 4, 8, 2), ("y", "x", "z", "core"))
    spec = P(None, ROW, COL)
    return jax.shard_map(
        body, mesh=finer, in_specs=(spec,), out_specs=spec, check_vma=False
    )
```

```python
import jax
import jax.numpy as jnp
from jax import lax
from jax.experimental import pallas as pl
from jax.experimental.pallas import tpu as pltpu
from jax.sharding import Mesh
from jax.sharding import PartitionSpec as P

PANELS = 2
HIGHEST = lax.Precision.HIGHEST
STEPS = 40
FAR_STEPS = 6
NEAR = 0.1
LAST = 5e-4
ROW = ("y", "x")
COL = ("z", "core")


together = lax.optimization_barrier


def doubled(block, axis, step):
    size = lax.axis_size(axis)
    pairs = [(i, i + step) for i in range(0, size, 2 * step)]
    sent = lax.ppermute(block, axis, pairs)
    return jnp.where(lax.axis_index(axis) % (2 * step) == step, sent, block)


def scattered(block, axis):
    size = lax.axis_size(axis)
    parts = jnp.split(block, size // 2)
    mine = jnp.where(lax.axis_index(axis) == 0, parts[0], 0.0)
    for i in range(1, size // 2):
        mine = mine + lax.ppermute(parts[i], axis, [(0, 2 * i)])
    return mine


def halved(block, axis):
    size = lax.axis_size(axis)
    keep, give = jnp.split(block, 2)
    sent = lax.ppermute(give, axis, [(i, i + 1) for i in range(0, size, 2)])
    return jnp.where(lax.axis_index(axis) % 2 == 1, sent, keep)


def gathered(block, axis):
    copies = jnp.broadcast_to(block, (lax.axis_size(axis), *block.shape))
    return lax.all_to_all(copies, axis, 0, 0)


def from_two(mine):
    x = lax.axis_index("x")
    near = lax.ppermute(mine, "x", [(0, 1), (1, 0)])
    even = lax.ppermute(mine, "x", [(0, 2), (1, 3)])
    odd = lax.ppermute(mine, "x", [(0, 3), (1, 2)])
    first = jnp.where(x == 0, mine, jnp.where(x == 1, near, jnp.where(x == 2, even, odd)))
    second = jnp.where(x == 1, mine, jnp.where(x == 0, near, jnp.where(x == 3, even, odd)))
    return jnp.concatenate([first, second])


def stacked(parts, tile):
    high, double, width = parts.shape
    parts = parts.reshape(high, 2, double // 2, width).transpose(1, 0, 2, 3)
    return parts.reshape(2 * tile, width)


def spread(choi):
    slots, tile, _ = choi.shape
    high = lax.axis_size("y")
    core = lax.axis_index("core")
    top = lax.all_to_all(choi[0].reshape(high, tile // high, tile), "y", 0, 0)[0]
    panel = scattered(choi.reshape(slots * tile, tile), "z")
    top = from_two(top)
    lead = doubled(top, "z", 4)
    panel, lead = together((panel, lead))
    panel = halved(panel, "z")
    column = gathered(top, "y")
    lead = doubled(lead, "z", 2)
    panel, lead = together((panel, lead))
    panels = lax.all_gather(panel, COL)
    lead = doubled(lead, "z", 1)
    lead, column = together((lead, column))
    lead = gathered(lead, "y")
    column, half = stacked(column, tile), stacked(lead, tile)
    pair = lax.ppermute(half, "core", [(0, 1), (1, 0)])
    left, right = jnp.where(core == 0, half, pair), jnp.where(core == 0, pair, half)
    lead = jnp.concatenate([left, right], axis=1)
    return column, lead, panels


def product(left, right, contract=((1,), (0,)), precision=HIGHEST):
    return lax.dot_general(
        left, right, (contract, ((), ())), precision=precision,
        preferred_element_type=jnp.float32,
    )


def coarse(left, right, contract=((1,), (0,))):
    return product(left.astype(jnp.bfloat16), right.astype(jnp.bfloat16), contract, None)


def rough(left, right, contract=((1,), (0,))):
    low = jnp.bfloat16
    left_high, right_high = left.astype(low), right.astype(low)
    left_rest = (left - left_high.astype(jnp.float32)).astype(low)
    right_rest = (right - right_high.astype(jnp.float32)).astype(low)
    small = product(left_high, right_rest, contract, None)
    small = small + product(left_rest, right_high, contract, None)
    return small + product(left_high, right_high, contract, None)


def square(block):
    return jnp.sum(block * block)


def eliminate(lead_ref, inverse_ref, work_ref):
    order = lead_ref.shape[0]
    rows = lax.broadcasted_iota(jnp.int32, (order, order), 0)
    cols = lax.broadcasted_iota(jnp.int32, (order, order), 1)
    work_ref[...] = lead_ref[...]
    inverse_ref[...] = (rows == cols).astype(jnp.float32)

    def pivot(k, carry):
        work = work_ref[...]
        column = jnp.sum(jnp.where(cols == k, work, 0.0), axis=1, keepdims=True)
        place = lax.broadcasted_iota(jnp.int32, (order, 1), 0)
        corner = jnp.sum(jnp.where(place == k, column, 0.0))
        scale = jnp.full((order, 1), corner)
        ratio = jnp.where(place > k, column / scale, 0.0)
        work_ref[...] = work - ratio * work_ref[pl.ds(k, 1), :]
        inverse = inverse_ref[...] - ratio * inverse_ref[pl.ds(k, 1), :]
        inverse_ref[...] = jnp.where(place == k, inverse / jnp.sqrt(scale), inverse)
        return carry

    lax.fori_loop(0, order, pivot, 0)


def update_kernel(
    place_ref, lead_ref, column_ref, panels_ref, choi_ref, out_ref, inverse_ref, work_ref, weight_ref, corner_ref
):
    order = lead_ref.shape[0]
    half = order // 2
    rows = lax.broadcasted_iota(jnp.int32, (order, order), 0)
    cols = lax.broadcasted_iota(jnp.int32, (order, order), 1)
    same = rows == cols
    lead = lead_ref[...]
    down = lax.rsqrt(jnp.sum(jnp.where(same, lead, 0.0), axis=1, keepdims=True))
    along = lax.rsqrt(jnp.sum(jnp.where(same, lead, 0.0), axis=0, keepdims=True))
    scaled = lead * down * along
    off = jnp.where(same, 0.0, scaled).astype(jnp.bfloat16)
    twice = product(off, off, precision=None)
    bound = jnp.sqrt(jnp.sqrt(jnp.full((1, 1), square(twice))))
    shrink = jnp.where(bound < 1.0, jnp.ones_like(bound), 1.0 / (1.0 + bound))
    first = jnp.where(rows > cols, -scaled * shrink, jnp.where(same, 1.5 - 0.5 * shrink, 0.0))
    inverse_ref[...] = first * along * jnp.sqrt(shrink)

    top, low = pl.ds(0, half), pl.ds(half, half)
    small_rows = rows[:half, :half]
    small_cols = cols[:half, :half]
    unit = (small_rows == small_cols).astype(jnp.float32)
    across = ((1,), (1,))

    def lower(block):
        return jnp.where(small_rows > small_cols, block, 0.5 * unit * block)

    def step(multiply):
        x00, x10, x11 = inverse_ref[top, top], inverse_ref[low, top], inverse_ref[low, low]
        s00, s10 = lead_ref[top, top], lead_ref[low, top]
        s01, s11 = lead_ref[top, low], lead_ref[low, low]
        y00 = multiply(x00, s00)
        y10 = multiply(x10, s00) + multiply(x11, s10)
        y11 = multiply(x10, s01) + multiply(x11, s11)
        e00 = multiply(y00, x00, across) - unit
        e10 = multiply(y10, x00, across)
        e11 = multiply(y10, x10, across) + multiply(y11, x11, across) - unit
        residual = jnp.sqrt(square(e00) + 2.0 * square(e10) + square(e11))
        f00, f11 = lower(e00), lower(e11)
        inverse_ref[top, top] = x00 - multiply(f00, x00)
        inverse_ref[low, top] = x10 - multiply(e10, x00) - multiply(f11, x10)
        inverse_ref[low, low] = x11 - multiply(f11, x11)
        return residual

    def far(carry):
        count, residual = carry
        return (count < FAR_STEPS) & (residual > NEAR)

    def unfinished(carry):
        count, residual = carry
        return (count < STEPS) & (residual > LAST)

    start = (jnp.int32(1), step(coarse))
    count, _ = lax.while_loop(far, lambda carry: (carry[0] + 1, step(rough)), start)
    start = (count, jnp.float32(1.0))
    _, residual = lax.while_loop(
        unfinished, lambda carry: (carry[0] + 1, step(product)), start
    )

    @pl.when(jnp.logical_not(residual <= LAST))
    def _():
        eliminate(lead_ref, inverse_ref, work_ref)

    x00, x10, x11 = inverse_ref[top, top], inverse_ref[low, top], inverse_ref[low, low]
    row, col = place_ref[0], place_ref[1]
    down = ((0,), (0,))

    @pl.when(col >= PANELS)
    def _():
        r0, r1 = column_ref[top, :], column_ref[low, :]
        h0 = product(x00, r0)
        h1 = product(x10, r0) + product(x11, r1)
        weight_ref[top, :] = product(x00, h0, down) + product(x10, h1, down)
        weight_ref[low, :] = product(x11, h1, down)
        corner_ref[...] = jnp.zeros((half, half), jnp.float32)

    @pl.when(col == 0)
    def _():
        weight_ref[top, :] = -x00.T
        weight_ref[low, :] = jnp.zeros((half, half), jnp.float32)
        corner = product(lead_ref[pl.ds(pl.multiple_of(jnp.minimum(row, 1) * half, half), half), top], x00, across)
        corner_ref[...] = jnp.where((row > 0) | (small_rows >= small_cols), corner, 0.0)

    @pl.when(col == 1)
    def _():
        weight_ref[top, :] = -x10.T
        weight_ref[low, :] = -x11.T
        corner = product(lead_ref[low, top], x10, across) + product(lead_ref[low, low], x11, across)
        corner_ref[...] = jnp.where((row > 0) & (small_rows >= small_cols), corner, 0.0)

    for slot in range(choi_ref.shape[0]):
        base = jnp.where(col < PANELS, 0.0, choi_ref[slot])
        for k in range(PANELS):
            panel = panels_ref[slot, :, k].reshape(half, half)
            base = base - product(panel, weight_ref[pl.ds(k * half, half), :])
        out_ref[slot] = base

    @pl.when(row < PANELS)
    def _():
        out_ref[0] = corner_ref[...]


def body(choi):
    slots, tile, _ = choi.shape
    order = PANELS * tile
    place = jnp.stack([lax.axis_index(ROW), lax.axis_index(COL)]).astype(jnp.int32)
    column, lead, panels = spread(choi)
    deep = panels.shape[0] // PANELS
    panels = panels.reshape(slots, deep // slots, PANELS, *panels.shape[1:])
    vector = pl.BlockSpec(memory_space=pltpu.VMEM)
    return pl.pallas_call(
        update_kernel,
        in_specs=[pl.BlockSpec(memory_space=pltpu.SMEM)] + [vector] * 4,
        out_specs=vector,
        out_shape=jax.ShapeDtypeStruct(choi.shape, jnp.float32),
        scratch_shapes=[
            pltpu.VMEM((order, order), jnp.float32),
            pltpu.VMEM((order, order), jnp.float32),
            pltpu.VMEM((order, tile), jnp.float32),
            pltpu.VMEM((tile, tile), jnp.float32),
        ],
        compiler_params=pltpu.CompilerParams(vmem_limit_bytes=32 * 2**20),
    )(place, lead, column, panels, choi)


def solution(mesh):
    finer = Mesh(mesh.devices.reshape(8, 4, 8, 2), ("y", "x", "z", "core"))
    spec = P(None, ROW, COL)
    return jax.shard_map(
        body, mesh=finer, in_specs=(spec,), out_specs=spec, check_vma=False
    )
```

```python
import jax
import jax.numpy as jnp
from jax import lax
from jax.experimental import pallas as pl
from jax.experimental.pallas import tpu as pltpu
from jax.sharding import Mesh
from jax.sharding import PartitionSpec as P

PANELS = 2
HIGHEST = lax.Precision.HIGHEST
STEPS = 40
FAR_STEPS = 6
NEAR = 0.1
LAST = 5e-4
ROW = ("y", "x")
COL = ("z", "core")


together = lax.optimization_barrier


def doubled(block, axis, step):
    size = lax.axis_size(axis)
    pairs = [(i, i + step) for i in range(0, size, 2 * step)]
    sent = lax.ppermute(block, axis, pairs)
    return jnp.where(lax.axis_index(axis) % (2 * step) == step, sent, block)


def scattered(block, axis):
    size = lax.axis_size(axis)
    parts = jnp.split(block, size // 2)
    mine = jnp.where(lax.axis_index(axis) == 0, parts[0], 0.0)
    for i in sorted(range(1, size // 2), key=lambda i: abs(2 * i - size // 2)):
        mine = mine + lax.ppermute(parts[i], axis, [(0, 2 * i)])
    return mine


def halved(block, axis):
    size = lax.axis_size(axis)
    keep, give = jnp.split(block, 2)
    sent = lax.ppermute(give, axis, [(i, i + 1) for i in range(0, size, 2)])
    return jnp.where(lax.axis_index(axis) % 2 == 1, sent, keep)


def gathered(block, axis):
    copies = jnp.broadcast_to(block, (lax.axis_size(axis), *block.shape))
    return lax.all_to_all(copies, axis, 0, 0)


def from_two(mine):
    x = lax.axis_index("x")
    near = lax.ppermute(mine, "x", [(0, 1), (1, 0)])
    even = lax.ppermute(mine, "x", [(0, 2), (1, 3)])
    odd = lax.ppermute(mine, "x", [(0, 3), (1, 2)])
    first = jnp.where(x == 0, mine, jnp.where(x == 1, near, jnp.where(x == 2, even, odd)))
    second = jnp.where(x == 1, mine, jnp.where(x == 0, near, jnp.where(x == 3, even, odd)))
    return jnp.concatenate([first, second])


def stacked(parts, tile):
    high, double, width = parts.shape
    parts = parts.reshape(high, 2, double // 2, width).transpose(1, 0, 2, 3)
    return parts.reshape(2 * tile, width)


def spread(choi):
    slots, tile, _ = choi.shape
    high = lax.axis_size("y")
    core = lax.axis_index("core")
    top = lax.all_to_all(choi[0].reshape(high, tile // high, tile), "y", 0, 0)[0]
    panel = scattered(choi.reshape(slots * tile, tile), "z")
    top = from_two(top)
    panel, top = together((panel, top))
    panel = halved(panel, "z")
    lead = doubled(top, "z", 4)
    panel, lead = together((panel, lead))
    panels = lax.all_gather(panel, COL)
    column = gathered(top, "y")
    lead = doubled(doubled(lead, "z", 2), "z", 1)
    lead, column = together((lead, column))
    lead = gathered(lead, "y")
    column, half = stacked(column, tile), stacked(lead, tile)
    pair = lax.ppermute(half, "core", [(0, 1), (1, 0)])
    left, right = jnp.where(core == 0, half, pair), jnp.where(core == 0, pair, half)
    lead = jnp.concatenate([left, right], axis=1)
    return column, lead, panels


def product(left, right, contract=((1,), (0,)), precision=HIGHEST):
    return lax.dot_general(
        left, right, (contract, ((), ())), precision=precision,
        preferred_element_type=jnp.float32,
    )


def coarse(left, right, contract=((1,), (0,))):
    return product(left.astype(jnp.bfloat16), right.astype(jnp.bfloat16), contract, None)


def rough(left, right, contract=((1,), (0,))):
    low = jnp.bfloat16
    left_high, right_high = left.astype(low), right.astype(low)
    left_rest = (left - left_high.astype(jnp.float32)).astype(low)
    right_rest = (right - right_high.astype(jnp.float32)).astype(low)
    small = product(left_high, right_rest, contract, None)
    small = small + product(left_rest, right_high, contract, None)
    return small + product(left_high, right_high, contract, None)


def square(block):
    return jnp.sum(block * block)


def eliminate(lead_ref, inverse_ref, work_ref):
    order = lead_ref.shape[0]
    rows = lax.broadcasted_iota(jnp.int32, (order, order), 0)
    cols = lax.broadcasted_iota(jnp.int32, (order, order), 1)
    work_ref[...] = lead_ref[...]
    inverse_ref[...] = (rows == cols).astype(jnp.float32)

    def pivot(k, carry):
        work = work_ref[...]
        column = jnp.sum(jnp.where(cols == k, work, 0.0), axis=1, keepdims=True)
        place = lax.broadcasted_iota(jnp.int32, (order, 1), 0)
        corner = jnp.sum(jnp.where(place == k, column, 0.0))
        scale = jnp.full((order, 1), corner)
        ratio = jnp.where(place > k, column / scale, 0.0)
        work_ref[...] = work - ratio * work_ref[pl.ds(k, 1), :]
        inverse = inverse_ref[...] - ratio * inverse_ref[pl.ds(k, 1), :]
        inverse_ref[...] = jnp.where(place == k, inverse / jnp.sqrt(scale), inverse)
        return carry

    lax.fori_loop(0, order, pivot, 0)


def update_kernel(
    place_ref, lead_ref, column_ref, panels_ref, choi_ref, out_ref, inverse_ref, work_ref, weight_ref, corner_ref
):
    order = lead_ref.shape[0]
    half = order // 2
    rows = lax.broadcasted_iota(jnp.int32, (order, order), 0)
    cols = lax.broadcasted_iota(jnp.int32, (order, order), 1)
    same = rows == cols
    lead = lead_ref[...]
    down = lax.rsqrt(jnp.sum(jnp.where(same, lead, 0.0), axis=1, keepdims=True))
    along = lax.rsqrt(jnp.sum(jnp.where(same, lead, 0.0), axis=0, keepdims=True))
    scaled = lead * down * along
    off = jnp.where(same, 0.0, scaled).astype(jnp.bfloat16)
    twice = product(off, off, precision=None)
    bound = jnp.sqrt(jnp.sqrt(jnp.full((1, 1), square(twice))))
    shrink = jnp.where(bound < 1.0, jnp.ones_like(bound), 1.0 / (1.0 + bound))
    first = jnp.where(rows > cols, -scaled * shrink, jnp.where(same, 1.5 - 0.5 * shrink, 0.0))
    inverse_ref[...] = first * along * jnp.sqrt(shrink)

    top, low = pl.ds(0, half), pl.ds(half, half)
    small_rows = rows[:half, :half]
    small_cols = cols[:half, :half]
    unit = (small_rows == small_cols).astype(jnp.float32)
    across = ((1,), (1,))

    def lower(block):
        return jnp.where(small_rows > small_cols, block, 0.5 * unit * block)

    def step(multiply):
        x00, x10, x11 = inverse_ref[top, top], inverse_ref[low, top], inverse_ref[low, low]
        s00, s10 = lead_ref[top, top], lead_ref[low, top]
        s01, s11 = lead_ref[top, low], lead_ref[low, low]
        y00 = multiply(x00, s00)
        y10 = multiply(x10, s00) + multiply(x11, s10)
        y11 = multiply(x10, s01) + multiply(x11, s11)
        e00 = multiply(y00, x00, across) - unit
        e10 = multiply(y10, x00, across)
        e11 = multiply(y10, x10, across) + multiply(y11, x11, across) - unit
        residual = jnp.sqrt(square(e00) + 2.0 * square(e10) + square(e11))
        f00, f11 = lower(e00), lower(e11)
        inverse_ref[top, top] = x00 - multiply(f00, x00)
        inverse_ref[low, top] = x10 - multiply(e10, x00) - multiply(f11, x10)
        inverse_ref[low, low] = x11 - multiply(f11, x11)
        return residual

    def far(carry):
        count, residual = carry
        return (count < FAR_STEPS) & (residual > NEAR)

    def unfinished(carry):
        count, residual = carry
        return (count < STEPS) & (residual > LAST)

    start = (jnp.int32(1), step(coarse))
    count, _ = lax.while_loop(far, lambda carry: (carry[0] + 1, step(rough)), start)
    start = (count, jnp.float32(1.0))
    _, residual = lax.while_loop(
        unfinished, lambda carry: (carry[0] + 1, step(product)), start
    )

    @pl.when(jnp.logical_not(residual <= LAST))
    def _():
        eliminate(lead_ref, inverse_ref, work_ref)

    x00, x10, x11 = inverse_ref[top, top], inverse_ref[low, top], inverse_ref[low, low]
    row, col = place_ref[0], place_ref[1]
    down = ((0,), (0,))

    @pl.when(col >= PANELS)
    def _():
        r0, r1 = column_ref[top, :], column_ref[low, :]
        h0 = product(x00, r0)
        h1 = product(x10, r0) + product(x11, r1)
        weight_ref[top, :] = product(x00, h0, down) + product(x10, h1, down)
        weight_ref[low, :] = product(x11, h1, down)
        corner_ref[...] = jnp.zeros((half, half), jnp.float32)

    @pl.when(col == 0)
    def _():
        weight_ref[top, :] = -x00.T
        weight_ref[low, :] = jnp.zeros((half, half), jnp.float32)
        corner = product(lead_ref[pl.ds(pl.multiple_of(jnp.minimum(row, 1) * half, half), half), top], x00, across)
        corner_ref[...] = jnp.where((row > 0) | (small_rows >= small_cols), corner, 0.0)

    @pl.when(col == 1)
    def _():
        weight_ref[top, :] = -x10.T
        weight_ref[low, :] = -x11.T
        corner = product(lead_ref[low, top], x10, across) + product(lead_ref[low, low], x11, across)
        corner_ref[...] = jnp.where((row > 0) & (small_rows >= small_cols), corner, 0.0)

    for slot in range(choi_ref.shape[0]):
        base = jnp.where(col < PANELS, 0.0, choi_ref[slot])
        for k in range(PANELS):
            panel = panels_ref[slot, :, k].reshape(half, half)
            base = base - product(panel, weight_ref[pl.ds(k * half, half), :])
        out_ref[slot] = base

    @pl.when(row < PANELS)
    def _():
        out_ref[0] = corner_ref[...]


def body(choi):
    slots, tile, _ = choi.shape
    order = PANELS * tile
    place = jnp.stack([lax.axis_index(ROW), lax.axis_index(COL)]).astype(jnp.int32)
    column, lead, panels = spread(choi)
    deep = panels.shape[0] // PANELS
    panels = panels.reshape(slots, deep // slots, PANELS, *panels.shape[1:])
    vector = pl.BlockSpec(memory_space=pltpu.VMEM)
    return pl.pallas_call(
        update_kernel,
        in_specs=[pl.BlockSpec(memory_space=pltpu.SMEM)] + [vector] * 4,
        out_specs=vector,
        out_shape=jax.ShapeDtypeStruct(choi.shape, jnp.float32),
        scratch_shapes=[
            pltpu.VMEM((order, order), jnp.float32),
            pltpu.VMEM((order, order), jnp.float32),
            pltpu.VMEM((order, tile), jnp.float32),
            pltpu.VMEM((tile, tile), jnp.float32),
        ],
        compiler_params=pltpu.CompilerParams(vmem_limit_bytes=32 * 2**20),
    )(place, lead, column, panels, choi)


def solution(mesh):
    finer = Mesh(mesh.devices.reshape(8, 4, 8, 2), ("y", "x", "z", "core"))
    spec = P(None, ROW, COL)
    return jax.shard_map(
        body, mesh=finer, in_specs=(spec,), out_specs=spec, check_vma=False
    )
```
